32 devices in a mesh: grp: 2 (over y), aux: 8 (over z, x), vec: 2 (over core).
Axes of the slice: x: 2, y: 2, z: 4, core: 2. Of those that a mesh axis runs over, the one named last changes fastest.
Arguments:
- trial: bfloat16 [8, 4736, 640], P(('grp', 'vec'), 'aux'), parts along dimension 0, may hold values from -6 to 6
- b_occ: bfloat16 [12, 640, 640], P('grp'), parts along dimension 0, may hold values from -0.0625 to 0.0625
- b_vir: bfloat16 [12, 4736, 4736], P('grp', 'aux'), parts along dimension 0, may hold values from -0.0625 to 0.0625
- b_mixed: bfloat16 [12, 4736, 640], P('grp', 'aux'), parts along dimension 0, may hold values from -0.0625 to 0.0625
- e_occ: float32 [1280], P('grp'), parts along dimension 0, may hold values from -1 to -0.3
- e_vir: float32 [9472], P(('grp', 'aux')), parts along dimension 0, may hold values from 0.05 to 1.5
- active: int32 [4], P('grp'), parts along dimension 0, may hold values from 0 to 3, as said below
Outputs:
- sigma: bfloat16 [8, 4736, 640], P(('grp', 'vec'), 'aux'), parts along dimension 0
The draws below stay inside these ranges and needn't reach their ends.
There are 2 independent parts, one for each index of `grp`. The reference program is written for one: setup_inputs(seed, part) draws one part's arguments, and reference() takes and returns one part's arrays. A program takes and returns all parts, laid end to end along the dimension named above; each array names one. Nothing has to cross between parts.
Inputs may be any that keep to these rules, and one draw needn't show every extreme that they name: `active`: 2 distinct trial-vector ids in increasing order; the last trial vector, 3, is always among them.
All inputs are finite; a program needn't handle non-finite values.
Results may differ from the reference program's by a relative error of at most 0.0023.
Values may be sent and summed in bfloat16 or wider, within the bound.
A program may use at most 128 MiB of HBM per device.

```python
import jax
import jax.numpy as jnp
from jax import lax

O = 640
V = 4736
AUX = 6
NVEC = 4
NACT = 2


def draw_active(key, part):
    key = jax.random.fold_in(key, 11)
    others = jax.random.permutation(key, NVEC - 1)[:NACT - 1].astype(jnp.int32)
    newest = jnp.full((1,), NVEC - 1, jnp.int32)
    return jnp.sort(jnp.concatenate([others, newest]))


def shard_levels(stream_key, extent, split, smallest, top_value):
    level = 1.0
    for axis_at, parts in split:
        draws = jax.random.uniform(jax.random.fold_in(jax.random.fold_in(stream_key, 6), axis_at), (parts,), jnp.float32, smallest / len(split), top_value / len(split))
        level = level * jnp.repeat(jnp.exp(draws), extent[axis_at] // parts).reshape((-1,) + (1,) * (len(extent) - 1 - axis_at))
    return level


def noise(rng, shape, width, bound, pieces=(), kind=jnp.bfloat16):
    gain = shard_levels(rng, shape, pieces, -0.22, 0.18) if pieces else 1.0
    drawn = jax.random.normal(rng, shape, jnp.float32) * width * gain
    return jnp.minimum(jnp.maximum(drawn, -bound), bound).astype(kind)


def setup_inputs(seed: int = 0, part: int = 0) -> dict:
    key_of = jax.random.split(jax.random.key(seed), 8)
    own_keys = jax.random.split(jax.random.fold_in(key_of[7], part), 8)
    trial = noise(own_keys[0], (NVEC, V, O), 1.0, 6.0, ((0, 2), (1, 8)))
    b_occ = noise(own_keys[1], (AUX, O, O), (2 * (AUX * O * V) ** 0.5) ** -0.5, 0.0625)
    b_vir = noise(own_keys[2], (AUX, V, V), (2 * (AUX * O * V) ** 0.5) ** -0.5, 0.0625, ((1, 8),))
    b_mixed = noise(own_keys[3], (AUX, V, O), (2 * (AUX * O * V) ** 0.5) ** -0.5, 0.0625, ((1, 8),))
    e_occ = jnp.clip(jax.random.uniform(own_keys[4], (O,), jnp.float32, -1.0, -0.3), -1.0, -0.3)
    e_vir = jnp.clip(0.05 + 1.45 * jax.random.uniform(own_keys[5], (V,), jnp.float32) ** shard_levels(own_keys[5], (V,), ((0, 8),), -0.2, 0.2), 0.05, 1.5)
    active = draw_active(jax.random.fold_in(jax.random.fold_in(key_of[7], part), 71), part)
    return {"trial": trial, "b_occ": b_occ, "b_vir": b_vir, "b_mixed": b_mixed, "e_occ": e_occ, "e_vir": e_vir, "active": active}


def reference(trial, b_occ, b_vir, b_mixed, e_occ, e_vir, active):
    chosen = jnp.take(trial, active.astype(jnp.int32), axis=0).astype(jnp.float32)
    high = lax.Precision.HIGHEST

    def one_fit(total, index):
        vir_part = b_vir[index].astype(jnp.float32)
        occ_part = b_occ[index].astype(jnp.float32)
        inner = jnp.einsum('ab,vbj->vaj', vir_part, chosen, precision=high)
        inner = inner.astype(jnp.bfloat16).astype(jnp.float32)
        return total + jnp.einsum('vaj,ij->vai', inner, occ_part, precision=high), None

    start = jnp.zeros(chosen.shape, jnp.float32)
    exch, _ = lax.scan(one_fit, start, jnp.arange(AUX, dtype=jnp.int32))
    mixed = b_mixed.astype(jnp.float32)
    fit = jnp.einsum('pbj,vbj->vp', mixed, chosen, precision=high)
    coul = jnp.einsum('vp,paj->vaj', fit, mixed, precision=high)
    gaps = e_vir[:, None] - e_occ[None, :]
    values = (gaps[None] * chosen + 2.0 * coul - exch).astype(jnp.bfloat16)
    result = jnp.zeros(trial.shape, jnp.bfloat16)
    return result.at[active.astype(jnp.int32)].set(values)
```

```python
import jax
import jax.numpy as jnp
from jax import lax
from jax.sharding import PartitionSpec as P


def products(chosen, b_occ, b_vir, b_mixed, e_occ, e_vir):
    partial_value = jnp.einsum("paj,aj->p", b_mixed, chosen, preferred_element_type=jnp.float32)
    every_row = lax.all_gather(chosen, "aux", axis=0, tiled=True)
    inner = jnp.einsum("pab,bj->paj", b_vir, every_row, preferred_element_type=jnp.float32)
    fit = lax.psum(partial_value, "aux")
    exch = jnp.einsum(
        "paj,pij->ai", inner.astype(jnp.bfloat16), b_occ, preferred_element_type=jnp.float32
    )
    coul = jnp.sum(fit[:, None, None] * b_mixed.astype(jnp.float32), axis=0)
    gaps = e_vir[:, None] - e_occ[None, :]
    return gaps * chosen.astype(jnp.float32) + 2.0 * coul - exch


def local(trial, b_occ, b_vir, b_mixed, e_occ, e_vir, active):
    core = lax.axis_index("vec")
    first = active[0]
    other = lax.ppermute(trial[0], "vec", [(1, 0)])
    lead = jnp.where(first == 0, trial[0], jnp.where(first == 1, trial[1], other))
    chosen = jnp.where(core == 0, lead, trial[1])
    values = products(chosen, b_occ, b_vir, b_mixed, e_occ, e_vir).astype(jnp.bfloat16)
    back = lax.ppermute(values, "vec", [(0, 1)])
    zero = jnp.zeros_like(values)
    slot0 = jnp.where(
        core == 0, jnp.where(first == 0, values, zero), jnp.where(first == 2, back, zero)
    )
    slot1 = jnp.where((core == 1) | (first == 1), values, zero)
    return jnp.stack([slot0, slot1])


def solution(mesh):
    in_specs = (
        P(("grp", "vec"), "aux", None),
        P("grp", None, None),
        P("grp", "aux", None),
        P("grp", "aux", None),
        P("grp"),
        P(("grp", "aux")),
        P("grp"),
    )
    out_specs = P(("grp", "vec"), "aux", None)
    return jax.shard_map(local, mesh=mesh, in_specs=in_specs, out_specs=out_specs, check_vma=False)
```

```python
import functools

import jax
import jax.numpy as jnp
from jax import lax
from jax.experimental import pallas as pl
from jax.experimental.pallas import tpu as pltpu
from jax.sharding import PartitionSpec as P

F32 = jnp.float32
BF16 = jnp.bfloat16
LANE = 128
STEP = 16
ZS, XS = 4, 2
ZX_CHUNKS = 5
SLOTS = 4
VISITS = (8, 10, 8, 4, 7)
LAST = VISITS[3] + VISITS[4]


def visit_starts(z, x):
    def pick(a, b, c, d):
        return jnp.where(z == 0, a, jnp.where(z == 1, b, jnp.where(z == 2, c, d)))

    first = pick(0, 10, 19, 29)
    second = pick(8, 0, 27, 19)
    third = pick(18, 18, 11, 11)
    low = pick(26, 26, 0, 0)
    early = low + jnp.where(x == 0, 0, VISITS[4])
    late = low + jnp.where(x == 0, VISITS[3], 0)
    return first, second, third, early, late


def visit_pairs(z):
    def pick(a, b, c, d):
        return jnp.where(z == 0, a, jnp.where(z == 1, b, jnp.where(z == 2, c, d)))

    return z, pick(1, 0, 3, 2), pick(2, 2, 1, 1), pick(3, 3, 0, 0)


def kernel(
    active, trial, b_occ, b_vir, b_mixed, e_occ, e_vir,
    mine, theirs,
    full, acc, occ, mixed, base, cand, vir, fits,
    load_sem, vir_sem, swap_send, swap_recv, back_send, back_recv, recv_sem, send_sem,
):
    aux = mixed.shape[0]
    rows, cols = mine.shape
    core = lax.axis_index("vec")
    at = lax.axis_index("aux")
    z, x = at // XS, at % XS
    step = 96
    tail = rows - ZX_CHUNKS * step
    XZ, FIT = ZX_CHUNKS, ZX_CHUNKS + 1

    loads = [
        pltpu.make_async_copy(trial.at[0], cand.at[0], load_sem.at[0]),
        pltpu.make_async_copy(trial.at[1], cand.at[1], load_sem.at[1]),
    ]
    load_mixed = pltpu.make_async_copy(b_mixed, mixed, load_sem.at[2])
    load_occ = pltpu.make_async_copy(b_occ, occ, load_sem.at[3])
    for load in loads:
        load.start()
    load_mixed.start()

    barrier = pltpu.get_barrier_semaphore()

    def greet(**where):
        pl.semaphore_signal(barrier, inc=1, device_id=where, device_id_type=pl.DeviceIdType.MESH)

    greet(vec=1 - core)
    greet(aux=z * XS + 1 - x)

    @pl.when(z < ZS - 1)
    def _():
        greet(aux=at + XS)

    @pl.when(z > 0)
    def _():
        greet(aux=at - XS)

    pl.semaphore_wait(barrier, 3 + jnp.where((z > 0) & (z < ZS - 1), 1, 0))

    swap = pltpu.make_async_remote_copy(
        src_ref=trial.at[0], dst_ref=cand.at[2], send_sem=swap_send, recv_sem=swap_recv,
        device_id={"vec": 1 - core}, device_id_type=pl.DeviceIdType.MESH,
    )

    @pl.when(core == 1)
    def _():
        swap.start()

    for load in loads:
        load.wait()

    @pl.when(core == 0)
    def _():
        swap.wait_recv()

    first = active[0]
    own = at * rows

    @pl.when(core == 1)
    def _():
        @pl.loop(0, rows // STEP)
        def _(r):
            here = pl.ds(pl.multiple_of(r * STEP, STEP), STEP)
            full[pl.ds(pl.multiple_of(own + r * STEP, STEP), STEP), :] = cand[1, here, :]

    @pl.when(core == 0)
    def _():
        @pl.loop(0, rows // STEP)
        def _(r):
            here = pl.ds(pl.multiple_of(r * STEP, STEP), STEP)
            a, b, c = cand[0, here, :], cand[1, here, :], cand[2, here, :]
            full[pl.ds(pl.multiple_of(own + r * STEP, STEP), STEP), :] = jnp.where(
                first == 0, a, jnp.where(first == 1, b, c)
            )

    def piece(block, m, kind):
        if kind == "fit":
            return fits.at[block]
        if kind == "xz":
            return full.at[pl.ds(pl.multiple_of(block * rows + ZX_CHUNKS * step, STEP), tail), :]
        return full.at[pl.ds(pl.multiple_of(block * rows + m * step, STEP), step), :]

    def index(m, kind):
        return FIT if kind == "fit" else XZ if kind == "xz" else m

    def copy(block, m, kind, way):
        target = (z * XS + 1 - x, at + XS, at - XS)[way]
        part, i = piece(block, m, kind), index(m, kind)
        return pltpu.make_async_remote_copy(
            src_ref=part, dst_ref=part,
            send_sem=send_sem.at[way, block, i], recv_sem=recv_sem.at[block, i],
            device_id={"aux": target}, device_id_type=pl.DeviceIdType.MESH,
        )

    def arrived(block, m, kind):
        copy(block, m, kind, 0).wait_recv()

    def pass_on(s, y_own, m, kind, act):
        block = s * XS + (x if y_own else 1 - x)
        if y_own:
            if kind == "xz":
                @pl.when(z == s)
                def _():
                    act(copy(block, m, kind, 0))
            else:
                act(copy(block, m, kind, 0))
        if y_own or kind == "xz":
            @pl.when((z >= s) & (z < ZS - 1))
            def _():
                act(copy(block, m, kind, 1))

            @pl.when((z <= s) & (z > 0))
            def _():
                act(copy(block, m, kind, 2))

    def start(c):
        c.start()

    def forward(d, m, kind):
        for s, there in ((z - d, z >= d), (z + d, z + d < ZS)):
            @pl.when(there)
            def _():
                arrived(s * XS + x, m, kind)
                pass_on(s, True, m, kind, start)
                if kind == "xz":
                    arrived(s * XS + 1 - x, m, kind)
                    pass_on(s, False, m, kind, start)

    def partner_chunks(s):
        @pl.loop(0, ZX_CHUNKS)
        def _(m):
            arrived(s * XS + 1 - x, m, "zx")

    pass_on(z, True, 0, "xz", start)

    @pl.loop(0, ZX_CHUNKS)
    def _(m):
        pass_on(z, True, m, "zx", start)

    starts = visit_starts(z, x)

    def fetch(v, p):
        width = VISITS[v] * LANE
        slot = (v * aux + p) % SLOTS
        return pltpu.make_async_copy(
            b_vir.at[p, :, pl.ds(pl.multiple_of(starts[v] * LANE, LANE), width)],
            vir.at[slot, :, pl.ds(0, width)],
            vir_sem.at[slot],
        )

    for p in range(SLOTS - 1):
        fetch(0, p).start()
    load_occ.start()

    load_mixed.wait()

    def fit_step(r, sums):
        here = pl.ds(pl.multiple_of(r * STEP, STEP), STEP)
        t = full[pl.ds(pl.multiple_of(own + r * STEP, STEP), STEP), :].astype(F32)
        new = []
        for p in range(aux):
            prod = mixed[p, here, :].astype(F32) * t
            prod = prod[:8] + prod[8:]
            new.append(
                sums[p] + sum(prod[:, k * LANE:(k + 1) * LANE] for k in range(cols // LANE))
            )
        return tuple(new)

    sums = lax.fori_loop(
        0, rows // STEP, fit_step, tuple(jnp.zeros((8, LANE), F32) for _ in range(aux))
    )
    for p in range(aux):
        fits[at, pl.ds(p, 1), :] = jnp.broadcast_to(jnp.sum(sums[p]).reshape(1, 1), (1, LANE))
    pass_on(z, True, 0, "fit", start)

    arrived(z * XS + 1 - x, 0, "xz")
    pass_on(z, False, 0, "xz", start)

    @pl.loop(0, ZX_CHUNKS)
    def _(m):
        forward(1, m, "zx")

    forward(1, 0, "xz")
    forward(1, 0, "fit")

    def visit(v, d):
        width = VISITS[v] * LANE
        begin = pl.multiple_of(starts[v] * LANE, LANE)

        @pl.loop(0, aux)
        def _(p):
            fetch(v, p).wait()

            @pl.when(p + SLOTS - 1 < aux)
            def _():
                fetch(v, p + SLOTS - 1).start()

            if v + 1 < len(VISITS):
                @pl.when(p + SLOTS - 1 >= aux)
                def _():
                    fetch(v + 1, p + SLOTS - 1 - aux).start()

            if d:
                @pl.when(p < ZX_CHUNKS)
                def _():
                    forward(d, p, "zx")

            part = jnp.dot(
                vir[(v * aux + p) % SLOTS, :, :width], full[pl.ds(begin, width), :],
                preferred_element_type=F32,
            )
            if v == 0:
                acc[p] = part
            else:
                acc[p] += part

        if d:
            forward(d, 0, "xz")
            forward(d, 0, "fit")

    pairs = visit_pairs(z)
    partner_chunks(pairs[0])
    visit(0, 2)
    partner_chunks(pairs[1])
    visit(1, 3)
    partner_chunks(pairs[2])
    visit(2, 0)

    for s in range(ZS):
        arrived(s * XS + 1 - x, 0, "fit")
    fit = fits[0]
    for b in range(1, ZS * XS):
        fit = fit + fits[b]

    @pl.loop(0, rows // STEP)
    def _(r):
        here = pl.ds(pl.multiple_of(r * STEP, STEP), STEP)
        t = full[pl.ds(pl.multiple_of(own + r * STEP, STEP), STEP), :].astype(F32)
        coul = fit[0:1, 0:1] * mixed[0, here, :].astype(F32)
        for p in range(1, aux):
            coul += fit[p:p + 1, 0:1] * mixed[p, here, :].astype(F32)
        base[here, :] = (e_vir[here, :] - e_occ[...]) * t + 2.0 * coul

    visit(3, 0)
    partner_chunks(pairs[3])
    visit(4, 0)

    load_occ.wait()
    half = (rows // 2 + STEP - 1) // STEP * STEP

    def back(k):
        here = pl.ds(0, half) if k == 0 else pl.ds(half, rows - half)
        return pltpu.make_async_remote_copy(
            src_ref=mine.at[here, :], dst_ref=theirs.at[here, :],
            send_sem=back_send.at[k], recv_sem=back_recv.at[k],
            device_id={"vec": 1 - core}, device_id_type=pl.DeviceIdType.MESH,
        )

    for k, here in enumerate((slice(0, half), slice(half, rows))):
        @pl.loop(0, aux)
        def _(p):
            base[here, :] -= lax.dot_general(
                acc[p, here, :].astype(BF16), occ[p], (((1,), (1,)), ((), ())),
                preferred_element_type=F32,
            )

        mine[here, :] = base[here, :].astype(BF16)

        @pl.when(core == 0)
        def _():
            back(k).start()

    def sent(c):
        c.wait_send()

    for s in range(ZS):
        @pl.loop(0, ZX_CHUNKS)
        def _(m):
            pass_on(s, True, m, "zx", sent)

        pass_on(s, True, 0, "xz", sent)
        pass_on(s, False, 0, "xz", sent)
        pass_on(s, True, 0, "fit", sent)

    @pl.when(core == 1)
    def _():
        swap.wait_send()
        for k in range(2):
            back(k).wait_recv()

    @pl.when(core == 0)
    def _():
        for k in range(2):
            back(k).wait_send()


def fused(trial, b_occ, b_vir, b_mixed, e_occ, e_vir, active):
    _, rows, cols = trial.shape
    aux, _, total = b_vir.shape
    blocks = ZS * XS
    widest = max(VISITS) * LANE
    hbm = pl.BlockSpec(memory_space=pl.ANY)
    vmem = pl.BlockSpec(memory_space=pltpu.VMEM)
    dma = pltpu.SemaphoreType.DMA
    block = jax.ShapeDtypeStruct((rows, cols), BF16)
    flops = 2 * aux * rows * cols * (total + cols)
    return pl.pallas_call(
        kernel,
        out_shape=(block, block),
        in_specs=[pl.BlockSpec(memory_space=pltpu.SMEM), hbm, hbm, hbm, hbm, vmem, vmem],
        out_specs=(vmem, vmem),
        scratch_shapes=[
            pltpu.VMEM((total, cols), BF16),
            pltpu.VMEM((aux, rows, cols), F32),
            pltpu.VMEM((aux, cols, cols), BF16),
            pltpu.VMEM((aux, rows, cols), BF16),
            pltpu.VMEM((rows, cols), F32),
            pltpu.VMEM((3, rows, cols), BF16),
            pltpu.VMEM((SLOTS, rows, widest), BF16),
            pltpu.VMEM((blocks, 8, LANE), F32),
            dma((4,)), dma((SLOTS,)), dma, dma, dma((2,)), dma((2,)),
            dma((blocks, ZX_CHUNKS + 2)), dma((3, blocks, ZX_CHUNKS + 2)),
        ],
        compiler_params=pltpu.CompilerParams(
            collective_id=0, has_side_effects=True, vmem_limit_bytes=56 * 2**20
        ),
        cost_estimate=pl.CostEstimate(
            flops=flops, bytes_accessed=2 * aux * rows * total, transcendentals=0
        ),
    )(active, trial, b_occ, b_vir, b_mixed, e_occ[None, :], e_vir[:, None])


def plain(trial, b_occ, b_vir, b_mixed, e_occ, e_vir, active):
    core = lax.axis_index("vec")
    first = active[0]
    other = lax.ppermute(trial[0], "vec", [(1, 0)])
    lead = jnp.where(first == 0, trial[0], jnp.where(first == 1, trial[1], other))
    chosen = jnp.where(core == 0, lead, trial[1])
    part = jnp.einsum("paj,aj->p", b_mixed, chosen, preferred_element_type=F32)
    every_row = lax.all_gather(chosen, "aux", axis=0, tiled=True)
    inner = jnp.einsum("pab,bj->paj", b_vir, every_row, preferred_element_type=F32)
    fit = lax.psum(part, "aux")
    exch = jnp.einsum("paj,pij->ai", inner.astype(BF16), b_occ, preferred_element_type=F32)
    coul = jnp.sum(fit[:, None, None] * b_mixed.astype(F32), axis=0)
    gaps = e_vir[:, None] - e_occ[None, :]
    values = (gaps * chosen.astype(F32) + 2.0 * coul - exch).astype(BF16)
    return values, lax.ppermute(values, "vec", [(0, 1)])


def local(small, trial, b_occ, b_vir, b_mixed, e_occ, e_vir, active):
    core = lax.axis_index("vec")
    first = active[0]
    work = fused if small and trial.shape[1] == 592 and trial.shape[2] == 640 else plain
    values, back = work(trial, b_occ, b_vir, b_mixed, e_occ, e_vir, active)
    zero = jnp.zeros_like(values)
    slot0 = jnp.where(
        core == 0, jnp.where(first == 0, values, zero), jnp.where(first == 2, back, zero)
    )
    slot1 = jnp.where((core == 1) | (first == 1), values, zero)
    return jnp.stack([slot0, slot1])


def solution(mesh):
    in_specs = (
        P(("grp", "vec"), "aux", None),
        P("grp", None, None),
        P("grp", "aux", None),
        P("grp", "aux", None),
        P("grp"),
        P(("grp", "aux")),
        P("grp"),
    )
    out_specs = P(("grp", "vec"), "aux", None)
    run = functools.partial(local, mesh.shape["aux"] == ZS * XS)
    return jax.shard_map(run, mesh=mesh, in_specs=in_specs, out_specs=out_specs, check_vma=False)
```
